512 devices in a mesh: met: 8 (over z), mach: 64 (over y, x, core).
Axes of the slice: x: 4, y: 8, z: 8, core: 2. Of those that a mesh axis runs over, the one named last changes fastest.
Arguments:
- tensor: float32 [4, 32768, 2048], P(None, 'mach', 'met'), may hold values from -6 to 6
- metric_factor: float32 [2048, 64], P(('met', 'mach')), may hold values from -0.125 to 0.125
- time_factor: float32 [4, 64], replicated, may hold values from 0.5 to 1.5
Outputs:
- machine_factor: float32 [32768, 64], P(('mach', 'met'))
- residual: float32 [4, 32768, 2048], P(None, 'mach', 'met')
The draws below stay inside these ranges and needn't reach their ends.
All inputs are finite; a program needn't handle non-finite values.
Results may differ from the reference program's by a relative error of at most 0.000078.
Values sent between devices are 32-bit elements; how exact they have to be, the bound alone decides.
No kernel may reach another device: no remote copies, remote signals or barrier semaphores. Data moves between devices by JAX's collectives and lax.ppermute only.
A program may use at most 64 MiB of HBM per device.

```python
import jax
import jax.numpy as jnp
from jax import lax

RANK = 64
STEPS = 4
METRICS = 2048
MACHINES = 32768


def shard_levels(rng, extent, pieces, smallest, high):
    factor_of = 1.0
    for position, shards_of in pieces:
        heights = jax.random.uniform(jax.random.fold_in(jax.random.fold_in(rng, 6), position), (shards_of,), jnp.float32, smallest / len(pieces), high / len(pieces))
        factor_of = factor_of * jnp.repeat(jnp.exp(heights), extent[position] // shards_of).reshape((-1,) + (1,) * (len(extent) - 1 - position))
    return factor_of


def bell_draw(rng, dims, scale, limit, cuts=(), held_as=jnp.bfloat16):
    gain = shard_levels(rng, dims, cuts, -0.22, 0.18) if cuts else 1.0
    drawn = jax.random.normal(rng, dims, jnp.float32) * scale * gain
    return jnp.minimum(jnp.maximum(drawn, -limit), limit).astype(held_as)


def setup_inputs(seed: int = 0) -> dict:
    seeds = jax.random.split(jax.random.key(seed), 4)
    tensor = bell_draw(seeds[0], (STEPS, MACHINES, METRICS), 1.0, 6.0, ((1, 64), (2, 8)), jnp.float32)
    metric_factor = bell_draw(seeds[1], (METRICS, RANK), METRICS ** -0.5, 0.125, ((0, 512),), jnp.float32)
    time_factor = jnp.clip(jax.random.uniform(seeds[2], (STEPS, RANK), jnp.float32, 0.5, 1.5), 0.5, 1.5)
    return {"tensor": tensor, "metric_factor": metric_factor, "time_factor": time_factor}


def reference(tensor, metric_factor, time_factor):
    highest = lax.Precision.HIGHEST
    khatri_rao = time_factor[:, None, :] * metric_factor[None, :, :]
    metric_gram = jnp.dot(metric_factor.T.astype(jnp.float32), metric_factor.astype(jnp.float32), precision=highest, preferred_element_type=jnp.float32)
    time_gram = jnp.dot(time_factor.T.astype(jnp.float32), time_factor.astype(jnp.float32), precision=highest, preferred_element_type=jnp.float32)
    normal_matrix = metric_gram * time_gram
    mttkrp = jnp.einsum('kij,kjr->ir', tensor, khatri_rao, precision=highest)
    cholesky_factor = jnp.linalg.cholesky(normal_matrix)
    machine_factor = jax.scipy.linalg.cho_solve((cholesky_factor, True), mttkrp.T).T
    rebuilt = jnp.einsum('ir,kjr->kij', machine_factor, khatri_rao, precision=highest)
    return (machine_factor, tensor - rebuilt)
```

```python
import jax
import jax.numpy as jnp
from jax import lax
from jax.experimental import pallas as pl
from jax.experimental.pallas import tpu as pltpu
from jax.sharding import PartitionSpec as P

RANK = 64
F32 = jnp.float32
BF16 = jnp.bfloat16
HIGHEST = lax.Precision.HIGHEST
LIMIT = 48 * 1024 * 1024
VMEM = pl.BlockSpec(memory_space=pltpu.VMEM)


def split(x):
    high = x.astype(BF16)
    return high, (x - high.astype(F32)).astype(BF16)


def dot(a, b, contract, precision=None):
    return lax.dot_general(
        a, b, (contract, ((), ())), precision=precision, preferred_element_type=F32
    )


def spread_kernel(m_ref, out_ref):
    rows = m_ref.shape[0]
    packed = jnp.concatenate(
        [
            jnp.concatenate([m_ref[i : i + 1, :], m_ref[i + 1 : i + 2, :]], axis=1)
            for i in range(0, rows, 2)
        ],
        axis=0,
    )
    out_ref[...] = jnp.broadcast_to(packed[None], out_ref.shape)


def sums_kernel(t_ref, g_ref, tf_ref, out_ref, m_ref):
    steps, machines, metrics = t_ref.shape
    parts = out_ref.shape[0]
    own = machines // parts
    half = own // 2
    m_ref[pl.ds(0, metrics // 2, stride=2), :] = g_ref[:, :RANK]
    m_ref[pl.ds(1, metrics // 2, stride=2), :] = g_ref[:, RANK:]
    m = m_ref[...]
    gram = dot(m, m, ((0,), (0,)), HIGHEST)
    gram = jnp.concatenate([gram[: RANK // 2], gram[RANK // 2 :]], axis=1)
    acc = jnp.zeros((machines, 2 * RANK), F32)
    for k in range(steps):
        right = jnp.concatenate(split(m * tf_ref[k : k + 1, :]), axis=1)
        high, low = split(t_ref[k])
        acc = acc + dot(high, right, ((1,), (0,))) + dot(low, right, ((1,), (0,)))
    for c in range(parts):
        block = acc[c * own : (c + 1) * own]
        sums = block[:, :RANK] + block[:, RANK:]
        out_ref[c, :half, :] = jnp.concatenate([sums[:half], sums[half:]], axis=1)
        out_ref[c, half:, :] = gram


def reduce_kernel(r_ref, own_ref, gram_ref):
    parts, rows, _ = r_ref.shape
    total = r_ref[0]
    for c in range(1, parts):
        total = total + r_ref[c]
    own_ref[...] = jnp.broadcast_to(total[None, : rows // 2], own_ref.shape)
    gram_ref[...] = total[rows // 2 :]


def solve_kernel(gram_ref, own_ref, m_ref, tf_ref, w_ref, rows_ref):
    steps = tf_ref.shape[0]
    packed = gram_ref[...]
    gram = jnp.concatenate([packed[:, :RANK], packed[:, RANK:]], axis=0)
    tf = tf_ref[...]
    normal = gram * dot(tf, tf, ((0,), (0,)), HIGHEST)
    row_id = lax.broadcasted_iota(jnp.int32, (RANK, RANK), 0)
    col_id = lax.broadcasted_iota(jnp.int32, (RANK, RANK), 1)
    both = jnp.concatenate([normal, (row_id == col_id).astype(F32)], axis=1)
    blocks = [both[8 * b : 8 * b + 8] for b in range(RANK // 8)]
    sub = lax.broadcasted_iota(jnp.int32, (8, 2 * RANK), 0)
    for j in range(RANK):
        b0, s = divmod(j, 8)
        row = blocks[b0][s : s + 1, :]
        scaled = row / row[:, j : j + 1]
        for b in range(b0, RANK // 8):
            column = jnp.broadcast_to(blocks[b][:, j : j + 1], (8, 2 * RANK))
            if b == b0:
                column = jnp.where(sub > s, column, 0.0)
            blocks[b] = blocks[b] - column * scaled
    done = jnp.concatenate(blocks, axis=0)
    left, right = done[:, :RANK], done[:, RANK:]
    pivots = jnp.sum(jnp.where(row_id == col_id, left, 0.0), axis=1, keepdims=True)
    inverse = right * lax.rsqrt(pivots)
    sums = jnp.concatenate([own_ref[0, :, :RANK], own_ref[0, :, RANK:]], axis=0)
    half = dot(sums, inverse, ((1,), (1,)), HIGHEST)
    rows_ref[...] = dot(half, inverse, ((1,), (0,)), HIGHEST)
    whole = dot(inverse, inverse, ((0,), (0,)), HIGHEST)
    m = m_ref[...]
    for k in range(steps):
        high, low = split(dot(whole, m * tf_ref[k : k + 1, :], ((1,), (1,)), HIGHEST))
        w_ref[k] = jnp.concatenate([high, high, low, low], axis=0)


def residual_kernel(t_ref, s_ref, w_ref, out_ref):
    packed = s_ref[...].reshape(s_ref.shape[0] * s_ref.shape[1], 2 * RANK)
    half = s_ref.shape[1]
    pieces = []
    for c in range(s_ref.shape[0]):
        block = packed[c * half : (c + 1) * half]
        pieces += [block[:, :RANK], block[:, RANK:]]
    high, low = split(jnp.concatenate(pieces, axis=0))
    left = jnp.concatenate([high, low, high, low], axis=1)
    for k in range(t_ref.shape[0]):
        out_ref[k] = t_ref[k] - dot(left, w_ref[k], ((1,), (0,)))


def local(parts, plane, tensor, metric_factor, time_factor):
    steps, machines, metrics = tensor.shape
    own = machines // parts
    params = pltpu.CompilerParams(vmem_limit_bytes=LIMIT)
    rows = metric_factor.shape[0]
    copies = pl.pallas_call(
        spread_kernel,
        out_shape=jax.ShapeDtypeStruct((plane, rows // 2, 2 * RANK), F32),
        in_specs=[VMEM],
        out_specs=VMEM,
    )(metric_factor)
    gathered = lax.all_to_all(copies, "mach", 0, 0).reshape(metrics // 2, 2 * RANK)
    partial, metric_block = pl.pallas_call(
        sums_kernel,
        out_shape=(
            jax.ShapeDtypeStruct((parts, own, 2 * RANK), F32),
            jax.ShapeDtypeStruct((metrics, RANK), F32),
        ),
        in_specs=[VMEM] * 3,
        out_specs=(VMEM, VMEM),
        compiler_params=params,
    )(tensor, gathered, time_factor)
    received = lax.all_to_all(partial, "met", 0, 0)
    own_sums, gram = pl.pallas_call(
        reduce_kernel,
        out_shape=(
            jax.ShapeDtypeStruct((parts, own // 2, 2 * RANK), F32),
            jax.ShapeDtypeStruct((RANK // 2, 2 * RANK), F32),
        ),
        in_specs=[VMEM],
        out_specs=(VMEM, VMEM),
    )(received)
    sums = lax.all_to_all(own_sums, "met", 0, 0)
    weights, own_rows = pl.pallas_call(
        solve_kernel,
        out_shape=(
            jax.ShapeDtypeStruct((steps, 4 * RANK, metrics), BF16),
            jax.ShapeDtypeStruct((own, RANK), F32),
        ),
        in_specs=[VMEM] * 4,
        out_specs=(VMEM, VMEM),
        compiler_params=params,
        cost_estimate=pl.CostEstimate(flops=10**9, bytes_accessed=10**7, transcendentals=0),
    )(gram, own_sums, metric_block, time_factor)
    residual = pl.pallas_call(
        residual_kernel,
        out_shape=jax.ShapeDtypeStruct(tensor.shape, F32),
        in_specs=[VMEM] * 3,
        out_specs=VMEM,
        compiler_params=params,
    )(tensor, sums, weights)
    return own_rows, residual


def solution(mesh):
    def run(tensor, metric_factor, time_factor):
        return local(mesh.shape["met"], mesh.shape["mach"], tensor, metric_factor, time_factor)

    return jax.shard_map(
        run,
        mesh=mesh,
        in_specs=(P(None, "mach", "met"), P(("met", "mach"), None), P()),
        out_specs=(P(("mach", "met"), None), P(None, "mach", "met")),
        check_vma=False,
    )
```

```python
import jax
import jax.numpy as jnp
from jax import lax
from jax.experimental import pallas as pl
from jax.experimental.pallas import tpu as pltpu
from jax.sharding import PartitionSpec as P

RANK = 64
F32 = jnp.float32
BF16 = jnp.bfloat16
HIGHEST = lax.Precision.HIGHEST
VMEM = pl.BlockSpec(memory_space=pltpu.VMEM)
PIECE = 128
PLANE_FIRST = 37
SUMS_FIRST = 7
ROWS_FIRST = 7


def params(mebibytes):
    return pltpu.CompilerParams(vmem_limit_bytes=mebibytes * 1024 * 1024)


def work(flops):
    return pl.CostEstimate(flops=flops, bytes_accessed=10**7, transcendentals=0)


def split(x):
    high = x.astype(BF16)
    return high, (x - high.astype(F32)).astype(BF16)


def dot(a, b, contract, precision=None):
    return lax.dot_general(
        a, b, (contract, ((), ())), precision=precision, preferred_element_type=F32
    )


def spread_kernel(m_ref, out_ref):
    rows = m_ref.shape[0]
    packed = jnp.concatenate(
        [
            jnp.concatenate([m_ref[i : i + 1, :], m_ref[i + 1 : i + 2, :]], axis=1)
            for i in range(0, rows, 2)
        ],
        axis=0,
    )
    out_ref[...] = jnp.broadcast_to(packed[None], out_ref.shape)


def prepare_kernel(t_ref, tf_ref, high_ref, low_ref, times_ref, gram_ref):
    for k in range(t_ref.shape[0]):
        high_ref[k], low_ref[k] = split(t_ref[k])
    tf = tf_ref[...]
    times_ref[...] = tf
    gram_ref[...] = dot(tf, tf, ((0,), (0,)), HIGHEST)


def sums_kernel(high_ref, low_ref, g_ref, tf_ref, out_ref, m_ref):
    steps, machines, metrics = high_ref.shape
    parts = out_ref.shape[0]
    own = machines // parts
    half = own // 2
    cut = 2 * PLANE_FIRST
    top = metrics // 2 - cut
    for h in range(2):
        lanes = slice(h * RANK, (h + 1) * RANK)
        m_ref[pl.ds(2 * cut + h, top, stride=2), :] = g_ref[:top, lanes]
        m_ref[pl.ds(h, cut, stride=2), :] = g_ref[top:, lanes]
    m = m_ref[...]
    gram = dot(m, m, ((0,), (0,)), HIGHEST)
    gram = jnp.concatenate([gram[: RANK // 2], gram[RANK // 2 :]], axis=1)
    acc = jnp.zeros((machines, 2 * RANK), F32)
    for k in range(steps):
        right = jnp.concatenate(split(m * tf_ref[k : k + 1, :]), axis=1)
        acc = acc + dot(high_ref[k], right, ((1,), (0,)))
        acc = acc + dot(low_ref[k], right, ((1,), (0,)))
    for i in range(parts):
        c = (i + SUMS_FIRST) % parts
        block = acc[c * own : (c + 1) * own]
        sums = block[:, :RANK] + block[:, RANK:]
        out_ref[i, :half, :] = jnp.concatenate([sums[:half], sums[half:]], axis=1)
        out_ref[i, half:, :] = gram


def reduce_kernel(r_ref, own_ref, gram_ref):
    parts, rows, _ = r_ref.shape
    total = r_ref[0]
    for c in range(1, parts):
        total = total + r_ref[c]
    own_ref[...] = jnp.broadcast_to(total[None, : rows // 2], own_ref.shape)
    gram_ref[...] = total[rows // 2 :]


def solve_kernel(gram_ref, own_ref, m_ref, tf_ref, times_ref, w_ref, rows_ref):
    steps = tf_ref.shape[0]
    packed = gram_ref[...]
    gram = jnp.concatenate([packed[:, :RANK], packed[:, RANK:]], axis=0)
    normal = gram * times_ref[...]
    row_id = lax.broadcasted_iota(jnp.int32, (RANK, RANK), 0)
    col_id = lax.broadcasted_iota(jnp.int32, (RANK, RANK), 1)
    both = jnp.concatenate([normal, (row_id == col_id).astype(F32)], axis=1)
    blocks = [both[8 * b : 8 * b + 8] for b in range(RANK // 8)]
    sub = lax.broadcasted_iota(jnp.int32, (8, 2 * RANK), 0)
    for j in range(RANK):
        b0, s = divmod(j, 8)
        row = blocks[b0][s : s + 1, :]
        scaled = row / row[:, j : j + 1]
        for b in range(b0, RANK // 8):
            column = jnp.broadcast_to(blocks[b][:, j : j + 1], (8, 2 * RANK))
            if b == b0:
                column = jnp.where(sub > s, column, 0.0)
            blocks[b] = blocks[b] - column * scaled
    done = jnp.concatenate(blocks, axis=0)
    left, right = done[:, :RANK], done[:, RANK:]
    pivots = jnp.sum(jnp.where(row_id == col_id, left, 0.0), axis=1, keepdims=True)
    inverse = right * lax.rsqrt(pivots)
    sums = jnp.concatenate([own_ref[0, :, :RANK], own_ref[0, :, RANK:]], axis=0)
    half = dot(sums, inverse, ((1,), (1,)), HIGHEST)
    rows_ref[...] = dot(half, inverse, ((1,), (0,)), HIGHEST)
    whole = dot(inverse, inverse, ((0,), (0,)), HIGHEST)
    m = m_ref[...]
    for k in range(steps):
        high, low = split(dot(whole, m * tf_ref[k : k + 1, :], ((1,), (1,)), HIGHEST))
        w_ref[k] = jnp.concatenate([high, high, low, low], axis=0)


def residual_kernel(t_ref, s_ref, w_ref, out_ref, held, sems):
    parts, half, _ = s_ref.shape
    steps, machines, _ = t_ref.shape
    copies = []
    per = PIECE // (2 * half)
    for p in range(machines // PIECE):
        pieces = []
        for c in range(p * per, (p + 1) * per):
            block = s_ref[(c - ROWS_FIRST) % parts]
            pieces += [block[:, :RANK], block[:, RANK:]]
        high, low = split(jnp.concatenate(pieces, axis=0))
        left = jnp.concatenate([high, low, high, low], axis=1)
        rows = pl.ds(p * PIECE, PIECE)
        for k in range(steps):
            held[k, rows, :] = t_ref[k, rows, :] - dot(left, w_ref[k], ((1,), (0,)))
            copy = pltpu.make_async_copy(
                held.at[k, rows, :], out_ref.at[k, rows, :], sems.at[p, k]
            )
            copy.start()
            copies.append(copy)
    for copy in copies:
        copy.wait()


def local(parts, plane, tensor, metric_factor, time_factor):
    steps, machines, metrics = tensor.shape
    own = machines // parts
    rows = metric_factor.shape[0]
    plane_order = [[(i + PLANE_FIRST) % plane for i in range(plane)]]
    sums_order = [[(i + SUMS_FIRST) % parts for i in range(parts)]]
    rows_order = [[(i + ROWS_FIRST) % parts for i in range(parts)]]
    copies = pl.pallas_call(
        spread_kernel,
        out_shape=jax.ShapeDtypeStruct((plane, rows // 2, 2 * RANK), F32),
        in_specs=[VMEM],
        out_specs=VMEM,
        compiler_params=params(2),
    )(metric_factor)
    gathered = lax.all_to_all(copies, "mach", 0, 0, axis_index_groups=plane_order).reshape(metrics // 2, 2 * RANK)
    high, low, times, time_gram = pl.pallas_call(
        prepare_kernel,
        out_shape=(
            jax.ShapeDtypeStruct(tensor.shape, BF16),
            jax.ShapeDtypeStruct(tensor.shape, BF16),
            jax.ShapeDtypeStruct(time_factor.shape, F32),
            jax.ShapeDtypeStruct((RANK, RANK), F32),
        ),
        in_specs=[VMEM] * 2,
        out_specs=(VMEM,) * 4,
        compiler_params=params(12),
        cost_estimate=work(10**9),
    )(tensor, time_factor)
    partial, metric_block = pl.pallas_call(
        sums_kernel,
        out_shape=(
            jax.ShapeDtypeStruct((parts, own, 2 * RANK), F32),
            jax.ShapeDtypeStruct((metrics, RANK), F32),
        ),
        in_specs=[VMEM] * 4,
        out_specs=(VMEM, VMEM),
        compiler_params=params(12),
    )(high, low, gathered, times)
    received = lax.all_to_all(partial, "met", 0, 0, axis_index_groups=sums_order)
    own_sums, gram = pl.pallas_call(
        reduce_kernel,
        out_shape=(
            jax.ShapeDtypeStruct((parts, own // 2, 2 * RANK), F32),
            jax.ShapeDtypeStruct((RANK // 2, 2 * RANK), F32),
        ),
        in_specs=[VMEM],
        out_specs=(VMEM, VMEM),
        compiler_params=params(4),
    )(received)
    sums = lax.all_to_all(own_sums, "met", 0, 0, axis_index_groups=rows_order)
    weights, own_rows = pl.pallas_call(
        solve_kernel,
        out_shape=(
            jax.ShapeDtypeStruct((steps, 4 * RANK, metrics), BF16),
            jax.ShapeDtypeStruct((own, RANK), F32),
        ),
        in_specs=[VMEM] * 5,
        out_specs=(VMEM, VMEM),
        compiler_params=params(8),
        cost_estimate=work(10**9),
    )(gram, own_sums, metric_block, times, time_gram)
    residual = pl.pallas_call(
        residual_kernel,
        out_shape=jax.ShapeDtypeStruct(tensor.shape, F32),
        in_specs=[VMEM] * 3,
        out_specs=pl.BlockSpec(memory_space=pl.ANY),
        scratch_shapes=[
            pltpu.VMEM(tensor.shape, F32),
            pltpu.SemaphoreType.DMA((machines // PIECE, steps)),
        ],
        compiler_params=params(12),
    )(tensor, sums, weights)
    return own_rows, residual


def solution(mesh):
    def run(tensor, metric_factor, time_factor):
        return local(mesh.shape["met"], mesh.shape["mach"], tensor, metric_factor, time_factor)

    return jax.shard_map(
        run,
        mesh=mesh,
        in_specs=(P(None, "mach", "met"), P(("met", "mach"), None), P()),
        out_specs=(P(("mach", "met"), None), P(None, "mach", "met")),
        check_vma=False,
    )
```

```python
import jax
import jax.numpy as jnp
from jax import lax
from jax.experimental import pallas as pl
from jax.experimental.pallas import tpu as pltpu
from jax.sharding import PartitionSpec as P

RANK = 64
F32 = jnp.float32
BF16 = jnp.bfloat16
HIGHEST = lax.Precision.HIGHEST
VMEM = pl.BlockSpec(memory_space=pltpu.VMEM)
PIECE = 128
FETCH = 256
GRAM = 3 * RANK // 8
PLANE_FIRST = 37
SUMS_ORDER = (6, 7, 0, 5, 1, 4, 2, 3)
ROWS_ORDER = (6, 7, 3, 1, 0, 2, 5, 4)


def params(mebibytes):
    return pltpu.CompilerParams(vmem_limit_bytes=mebibytes * 1024 * 1024)


def work(flops):
    return pl.CostEstimate(flops=flops, bytes_accessed=10**7, transcendentals=0)


def split(x):
    high = x.astype(BF16)
    return high, (x - high.astype(F32)).astype(BF16)


def dot(a, b, contract, precision=None):
    return lax.dot_general(
        a, b, (contract, ((), ())), precision=precision, preferred_element_type=F32
    )


def spread_kernel(m_ref, out_ref):
    rows = m_ref.shape[0]
    packed = jnp.concatenate(
        [
            jnp.concatenate([m_ref[i : i + 1, :], m_ref[i + 1 : i + 2, :]], axis=1)
            for i in range(0, rows, 2)
        ],
        axis=0,
    )
    out_ref[...] = jnp.broadcast_to(packed[None], out_ref.shape)


def fetch_kernel(t_hbm, tf_hbm, t_ref, tf_ref, gram_ref, sems, tf_sem):
    small = pltpu.make_async_copy(tf_hbm, tf_ref, tf_sem)
    small.start()
    copies = []
    steps, machines, _ = t_ref.shape
    for k in range(steps):
        for p in range(machines // FETCH):
            rows = pl.ds(p * FETCH, FETCH)
            copies.append(
                pltpu.make_async_copy(t_hbm.at[k, rows, :], t_ref.at[k, rows, :], sems.at[k, p])
            )
            copies[-1].start()
    small.wait()
    tf = tf_ref[...]
    gram_ref[...] = dot(tf, tf, ((0,), (0,)), HIGHEST)
    for copy in copies:
        copy.wait()


def pack_gram(gram):
    half = RANK // 2
    rows = [gram[8 * i : 8 * i + 8] for i in range(RANK // 8)]
    return jnp.concatenate(
        [
            jnp.concatenate(rows[0:2], axis=1),
            jnp.concatenate(rows[2:4], axis=1),
            jnp.concatenate([row[:, half:] for row in rows[4:]], axis=1),
        ],
        axis=0,
    )


def unpack_gram(packed):
    half = RANK // 2
    top = jnp.concatenate(
        [packed[i : i + 8, h : h + RANK] for i in (0, 8) for h in (0, RANK)], axis=0
    )
    corner = jnp.concatenate(
        [packed[16:24, half * i : half * (i + 1)] for i in range(4)], axis=0
    )
    bottom = jnp.concatenate([top[:, half:].T, corner], axis=1)
    return jnp.concatenate([top, bottom], axis=0)


def sums_kernel(t_ref, g_ref, tf_ref, out_ref, m_ref):
    steps, machines, metrics = t_ref.shape
    parts = out_ref.shape[0]
    own = machines // parts
    half = own // 2
    cut = 2 * PLANE_FIRST
    top = metrics // 2 - cut
    for h in range(2):
        lanes = slice(h * RANK, (h + 1) * RANK)
        m_ref[pl.ds(2 * cut + h, top, stride=2), :] = g_ref[:top, lanes]
        m_ref[pl.ds(h, cut, stride=2), :] = g_ref[top:, lanes]
    m = m_ref[...]
    gram = pack_gram(dot(m, m, ((0,), (0,)), HIGHEST))
    acc = jnp.zeros((machines, 2 * RANK), F32)
    for k in range(steps):
        right = jnp.concatenate(split(m * tf_ref[k : k + 1, :]), axis=1)
        high, low = split(t_ref[k])
        acc = acc + (dot(high, right, ((1,), (0,))) + dot(low, right, ((1,), (0,))))
    for i in range(parts):
        c = SUMS_ORDER[i]
        block = acc[c * own : (c + 1) * own]
        sums = block[:, :RANK] + block[:, RANK:]
        out_ref[i, :half, :] = jnp.concatenate([sums[:half], sums[half:]], axis=1)
        out_ref[i, half:, :] = gram


def reduce_kernel(r_ref, own_ref, gram_ref):
    parts, rows, _ = own_ref.shape
    total = r_ref[0]
    for c in range(1, parts):
        total = total + r_ref[c]
    own_ref[...] = jnp.broadcast_to(total[None, :rows], own_ref.shape)
    gram_ref[...] = total[rows:]


def inverse_factor(normal):
    wide = 2 * RANK
    count = RANK // 8
    row_id = lax.broadcasted_iota(jnp.int32, (RANK, RANK), 0)
    col_id = lax.broadcasted_iota(jnp.int32, (RANK, RANK), 1)
    both = jnp.concatenate([normal, (row_id == col_id).astype(F32)], axis=1)
    blocks = [both[8 * b : 8 * b + 8] for b in range(count)]
    sub = lax.broadcasted_iota(jnp.int32, (8, wide), 0)

    def column(x, j):
        return jnp.broadcast_to(x[:, j : j + 1], (8, wide))

    def row(x, i):
        return jnp.broadcast_to(x[i : i + 1, :], (8, wide))

    done = []
    for b in range(count):
        panel = blocks[b]
        columns = [column(panel, 8 * b + t) for t in range(8)]
        entry = {(s, t): row(columns[t], s) for s in range(8) for t in range(s, 8)}
        upper = [row(panel, t) for t in range(8)]
        below = {
            i: [column(blocks[i], 8 * b + t) for t in range(8)] for i in range(b + 1, count)
        }
        rows = panel
        for s in range(0, 8, 2):
            v = s + 1
            a, o, d = entry[s, s], entry[s, v], entry[v, v]
            inverse = 1.0 / (a * d - o * o)
            later = range(s + 2, 8)
            first = {t: (entry[s, t] * d - entry[v, t] * o) * inverse for t in later}
            second = {t: (entry[v, t] * a - entry[s, t] * o) * inverse for t in later}
            upper_first = (upper[s] * d - upper[v] * o) * inverse
            upper_second = (upper[v] * a - upper[s] * o) * inverse
            for t in later:
                for q in range(t, 8):
                    entry[t, q] -= first[t] * entry[s, q] + second[t] * entry[v, q]
                upper[t] = upper[t] - (first[t] * upper[s] + second[t] * upper[v])
            for i, side in below.items():
                blocks[i] = blocks[i] - (side[s] * upper_first + side[v] * upper_second)
                for t in later:
                    side[t] = side[t] - (first[t] * side[s] + second[t] * side[v])
            ratio = o / a
            rows = jnp.where(sub == s, upper[s] * lax.rsqrt(a), rows)
            last = (upper[v] - ratio * upper[s]) * lax.rsqrt(d - o * ratio)
            rows = jnp.where(sub == v, last, rows)
        done.append(rows)
    return jnp.concatenate(done, axis=0)[:, RANK:]


def solve_kernel(gram_ref, own_ref, m_ref, tf_ref, times_ref, w_ref, rows_ref):
    inverse = inverse_factor(unpack_gram(gram_ref[...]) * times_ref[...])
    whole = dot(inverse, inverse, ((0,), (0,)), HIGHEST)
    sums = jnp.concatenate([own_ref[0, :, :RANK], own_ref[0, :, RANK:]], axis=0)
    rows_ref[...] = dot(sums, whole, ((1,), (0,)), HIGHEST)
    high, low = split(whole)
    left = jnp.concatenate([high, low, high, low], axis=1)
    m = m_ref[...]
    for k in range(tf_ref.shape[0]):
        high, low = split(m * tf_ref[k : k + 1, :])
        right = jnp.concatenate([high, high, low, low], axis=1)
        high, low = split(dot(left, right, ((1,), (1,))))
        w_ref[k] = jnp.concatenate([high, high, low, low], axis=0)


def residual_kernel(t_ref, s_ref, w_ref, out_ref, held, sems):
    parts, half, _ = s_ref.shape
    steps, machines, _ = t_ref.shape
    copies = []
    per = PIECE // (2 * half)
    for p in range(machines // PIECE):
        pieces = []
        for c in range(p * per, (p + 1) * per):
            block = s_ref[ROWS_ORDER.index(c)]
            pieces += [block[:, :RANK], block[:, RANK:]]
        high, low = split(jnp.concatenate(pieces, axis=0))
        left = jnp.concatenate([high, low, high, low], axis=1)
        rows = pl.ds(p * PIECE, PIECE)
        for k in range(steps):
            held[k, rows, :] = t_ref[k, rows, :] - dot(left, w_ref[k], ((1,), (0,)))
            copy = pltpu.make_async_copy(
                held.at[k, rows, :], out_ref.at[k, rows, :], sems.at[p, k]
            )
            copy.start()
            copies.append(copy)
    for copy in copies:
        copy.wait()


def local(parts, plane, tensor, metric_factor, time_factor):
    steps, machines, metrics = tensor.shape
    own = machines // parts
    rows = metric_factor.shape[0]
    plane_order = [[(i + PLANE_FIRST) % plane for i in range(plane)]]
    copies = pl.pallas_call(
        spread_kernel,
        out_shape=jax.ShapeDtypeStruct((plane, rows // 2, 2 * RANK), F32),
        in_specs=[VMEM],
        out_specs=VMEM,
        compiler_params=params(2),
    )(metric_factor)
    gathered = lax.all_to_all(copies, "mach", 0, 0, axis_index_groups=plane_order).reshape(metrics // 2, 2 * RANK)
    held, times, time_gram = pl.pallas_call(
        fetch_kernel,
        out_shape=(
            jax.ShapeDtypeStruct(tensor.shape, F32),
            jax.ShapeDtypeStruct(time_factor.shape, F32),
            jax.ShapeDtypeStruct((RANK, RANK), F32),
        ),
        in_specs=[pl.BlockSpec(memory_space=pltpu.HBM)] * 2,
        out_specs=(VMEM,) * 3,
        scratch_shapes=[
            pltpu.SemaphoreType.DMA((steps, machines // FETCH)),
            pltpu.SemaphoreType.DMA,
        ],
        compiler_params=params(12),
        cost_estimate=work(10**9),
    )(
        pltpu.with_memory_space_constraint(tensor, pltpu.HBM),
        pltpu.with_memory_space_constraint(time_factor, pltpu.HBM),
    )
    half = own // 2
    partial, metric_block = pl.pallas_call(
        sums_kernel,
        out_shape=(
            jax.ShapeDtypeStruct((parts, half + GRAM, 2 * RANK), F32),
            jax.ShapeDtypeStruct((metrics, RANK), F32),
        ),
        in_specs=[VMEM] * 3,
        out_specs=(VMEM, VMEM),
        compiler_params=params(12),
    )(held, gathered, times)
    received = lax.all_to_all(partial, "met", 0, 0, axis_index_groups=[SUMS_ORDER])
    own_sums, gram = pl.pallas_call(
        reduce_kernel,
        out_shape=(
            jax.ShapeDtypeStruct((parts, half, 2 * RANK), F32),
            jax.ShapeDtypeStruct((GRAM, 2 * RANK), F32),
        ),
        in_specs=[VMEM],
        out_specs=(VMEM, VMEM),
        compiler_params=params(4),
    )(received)
    sums = lax.all_to_all(own_sums, "met", 0, 0, axis_index_groups=[ROWS_ORDER])
    weights, own_rows = pl.pallas_call(
        solve_kernel,
        out_shape=(
            jax.ShapeDtypeStruct((steps, 4 * RANK, metrics), BF16),
            jax.ShapeDtypeStruct((own, RANK), F32),
        ),
        in_specs=[VMEM] * 5,
        out_specs=(VMEM, VMEM),
        compiler_params=params(8),
        cost_estimate=work(10**9),
    )(gram, own_sums, metric_block, times, time_gram)
    residual = pl.pallas_call(
        residual_kernel,
        out_shape=jax.ShapeDtypeStruct(tensor.shape, F32),
        in_specs=[VMEM] * 3,
        out_specs=pl.BlockSpec(memory_space=pl.ANY),
        scratch_shapes=[
            pltpu.VMEM(tensor.shape, F32),
            pltpu.SemaphoreType.DMA((machines // PIECE, steps)),
        ],
        compiler_params=params(12),
    )(held, sums, weights)
    return own_rows, residual


def solution(mesh):
    def run(tensor, metric_factor, time_factor):
        return local(mesh.shape["met"], mesh.shape["mach"], tensor, metric_factor, time_factor)

    return jax.shard_map(
        run,
        mesh=mesh,
        in_specs=(P(None, "mach", "met"), P(("met", "mach"), None), P()),
        out_specs=(P(("mach", "met"), None), P(None, "mach", "met")),
        check_vma=False,
    )
```

```python
import jax
import jax.numpy as jnp
from jax import lax
from jax.experimental import pallas as pl
from jax.experimental.pallas import tpu as pltpu
from jax.sharding import PartitionSpec as P

RANK = 64
F32 = jnp.float32
BF16 = jnp.bfloat16
HIGHEST = lax.Precision.HIGHEST
VMEM = pl.BlockSpec(memory_space=pltpu.VMEM)
PIECE = 128
FETCH = 256
GRAM = 3 * RANK // 8
PLANE_FIRST = 37
SUMS_ORDER = (6, 7, 0, 5, 1, 4, 2, 3)
ROWS_ORDER = (6, 7, 3, 1, 0, 2, 5, 4)


def params(mebibytes):
    return pltpu.CompilerParams(vmem_limit_bytes=mebibytes * 1024 * 1024)


def work(flops):
    return pl.CostEstimate(flops=flops, bytes_accessed=10**7, transcendentals=0)


def split(x):
    high = x.astype(BF16)
    return high, (x - high.astype(F32)).astype(BF16)


def dot(a, b, contract, precision=None):
    return lax.dot_general(
        a, b, (contract, ((), ())), precision=precision, preferred_element_type=F32
    )


def begin_kernel(m_hbm, t_hbm, tf_hbm, out_ref, t_ref, tf_ref, gram_ref, m_ref, sems, m_sem, tf_sem):
    first = pltpu.make_async_copy(m_hbm, m_ref, m_sem)
    first.start()
    small = pltpu.make_async_copy(tf_hbm, tf_ref, tf_sem)
    small.start()
    copies = []
    steps, machines, _ = t_ref.shape
    for k in range(steps):
        for p in range(machines // FETCH):
            rows = pl.ds(p * FETCH, FETCH)
            copies.append(
                pltpu.make_async_copy(t_hbm.at[k, rows, :], t_ref.at[k, rows, :], sems.at[k, p])
            )
            copies[-1].start()
    first.wait()
    packed = jnp.concatenate(
        [
            jnp.concatenate([m_ref[i : i + 1, :], m_ref[i + 1 : i + 2, :]], axis=1)
            for i in range(0, m_ref.shape[0], 2)
        ],
        axis=0,
    )
    out_ref[...] = jnp.broadcast_to(packed[None], out_ref.shape)
    small.wait()
    tf = tf_ref[...]
    gram_ref[...] = dot(tf, tf, ((0,), (0,)), HIGHEST)
    for copy in copies:
        copy.wait()


def pack_gram(gram):
    half = RANK // 2
    rows = [gram[8 * i : 8 * i + 8] for i in range(RANK // 8)]
    return jnp.concatenate(
        [
            jnp.concatenate(rows[0:2], axis=1),
            jnp.concatenate(rows[2:4], axis=1),
            jnp.concatenate([row[:, half:] for row in rows[4:]], axis=1),
        ],
        axis=0,
    )


def unpack_gram(packed):
    half = RANK // 2
    top = jnp.concatenate(
        [packed[i : i + 8, h : h + RANK] for i in (0, 8) for h in (0, RANK)], axis=0
    )
    corner = jnp.concatenate(
        [packed[16:24, half * i : half * (i + 1)] for i in range(4)], axis=0
    )
    bottom = jnp.concatenate([top[:, half:].T, corner], axis=1)
    return jnp.concatenate([top, bottom], axis=0)


def sums_kernel(t_ref, g_ref, tf_ref, out_ref, m_ref):
    steps, machines, metrics = t_ref.shape
    parts = out_ref.shape[0]
    own = machines // parts
    half = own // 2
    cut = 2 * PLANE_FIRST
    top = metrics // 2 - cut
    for h in range(2):
        lanes = slice(h * RANK, (h + 1) * RANK)
        m_ref[pl.ds(2 * cut + h, top, stride=2), :] = g_ref[:top, lanes]
        m_ref[pl.ds(h, cut, stride=2), :] = g_ref[top:, lanes]
    m = m_ref[...]
    gram = pack_gram(dot(m, m, ((0,), (0,)), HIGHEST))
    acc = jnp.zeros((machines, 2 * RANK), F32)
    for k in range(steps):
        right = jnp.concatenate(split(m * tf_ref[k : k + 1, :]), axis=1)
        high, low = split(t_ref[k])
        acc = acc + (dot(high, right, ((1,), (0,))) + dot(low, right, ((1,), (0,))))
    for i in range(parts):
        c = SUMS_ORDER[i]
        block = acc[c * own : (c + 1) * own]
        sums = block[:, :RANK] + block[:, RANK:]
        out_ref[i, :half, :] = jnp.concatenate([sums[:half], sums[half:]], axis=1)
        out_ref[i, half:, :] = gram


def reduce_kernel(r_ref, own_ref, gram_ref):
    parts, rows, _ = own_ref.shape
    total = r_ref[0]
    for c in range(1, parts):
        total = total + r_ref[c]
    own_ref[...] = jnp.broadcast_to(total[None, :rows], own_ref.shape)
    gram_ref[...] = total[rows:]


def inverse_factor(normal):
    wide = 2 * RANK
    count = RANK // 8
    row_id = lax.broadcasted_iota(jnp.int32, (RANK, RANK), 0)
    col_id = lax.broadcasted_iota(jnp.int32, (RANK, RANK), 1)
    both = jnp.concatenate([normal, (row_id == col_id).astype(F32)], axis=1)
    blocks = [both[8 * b : 8 * b + 8] for b in range(count)]
    sub = lax.broadcasted_iota(jnp.int32, (8, wide), 0)

    def column(x, j):
        return jnp.broadcast_to(x[:, j : j + 1], (8, wide))

    def row(x, i):
        return jnp.broadcast_to(x[i : i + 1, :], (8, wide))

    done = []
    for b in range(count):
        panel = blocks[b]
        columns = [column(panel, 8 * b + t) for t in range(8)]
        entry = {(s, t): row(columns[t], s) for s in range(8) for t in range(s, 8)}
        upper = [row(panel, t) for t in range(8)]
        below = {
            i: [column(blocks[i], 8 * b + t) for t in range(8)] for i in range(b + 1, count)
        }
        rows = panel
        for s in range(0, 8, 2):
            v = s + 1
            a, o, d = entry[s, s], entry[s, v], entry[v, v]
            inverse = 1.0 / (a * d - o * o)
            later = range(s + 2, 8)
            first = {t: (entry[s, t] * d - entry[v, t] * o) * inverse for t in later}
            second = {t: (entry[v, t] * a - entry[s, t] * o) * inverse for t in later}
            upper_first = (upper[s] * d - upper[v] * o) * inverse
            upper_second = (upper[v] * a - upper[s] * o) * inverse
            for t in later:
                for q in range(t, 8):
                    entry[t, q] -= first[t] * entry[s, q] + second[t] * entry[v, q]
                upper[t] = upper[t] - (first[t] * upper[s] + second[t] * upper[v])
            for i, side in below.items():
                blocks[i] = blocks[i] - (side[s] * upper_first + side[v] * upper_second)
                for t in later:
                    side[t] = side[t] - (first[t] * side[s] + second[t] * side[v])
            ratio = o / a
            rows = jnp.where(sub == s, upper[s] * lax.rsqrt(a), rows)
            last = (upper[v] - ratio * upper[s]) * lax.rsqrt(d - o * ratio)
            rows = jnp.where(sub == v, last, rows)
        done.append(rows)
    return jnp.concatenate(done, axis=0)[:, RANK:]


def solve_kernel(gram_ref, own_ref, m_ref, tf_ref, times_ref, w_ref, rows_ref):
    inverse = inverse_factor(unpack_gram(gram_ref[...]) * times_ref[...])
    whole = dot(inverse, inverse, ((0,), (0,)), HIGHEST)
    sums = jnp.concatenate([own_ref[0, :, :RANK], own_ref[0, :, RANK:]], axis=0)
    rows_ref[...] = dot(sums, whole, ((1,), (0,)), HIGHEST)
    high, low = split(whole)
    left = jnp.concatenate([high, low, high, low], axis=1)
    m = m_ref[...]
    for k in range(tf_ref.shape[0]):
        high, low = split(m * tf_ref[k : k + 1, :])
        right = jnp.concatenate([high, high, low, low], axis=1)
        high, low = split(dot(left, right, ((1,), (1,))))
        w_ref[k] = jnp.concatenate([high, high, low, low], axis=0)


def residual_kernel(t_ref, s_ref, w_ref, out_ref, held, sems):
    parts, half, _ = s_ref.shape
    steps, machines, _ = t_ref.shape
    copies = []
    per = PIECE // (2 * half)
    for p in range(machines // PIECE):
        pieces = []
        for c in range(p * per, (p + 1) * per):
            block = s_ref[ROWS_ORDER.index(c)]
            pieces += [block[:, :RANK], block[:, RANK:]]
        high, low = split(jnp.concatenate(pieces, axis=0))
        left = jnp.concatenate([high, low, high, low], axis=1)
        rows = pl.ds(p * PIECE, PIECE)
        for k in range(steps):
            held[k, rows, :] = t_ref[k, rows, :] - dot(left, w_ref[k], ((1,), (0,)))
            copy = pltpu.make_async_copy(
                held.at[k, rows, :], out_ref.at[k, rows, :], sems.at[p, k]
            )
            copy.start()
            copies.append(copy)
    for copy in copies:
        copy.wait()


def local(parts, plane, tensor, metric_factor, time_factor):
    steps, machines, metrics = tensor.shape
    own = machines // parts
    rows = metric_factor.shape[0]
    plane_order = [[(i + PLANE_FIRST) % plane for i in range(plane)]]
    copies, held, times, time_gram = pl.pallas_call(
        begin_kernel,
        out_shape=(
            jax.ShapeDtypeStruct((plane, rows // 2, 2 * RANK), F32),
            jax.ShapeDtypeStruct(tensor.shape, F32),
            jax.ShapeDtypeStruct(time_factor.shape, F32),
            jax.ShapeDtypeStruct((RANK, RANK), F32),
        ),
        in_specs=[pl.BlockSpec(memory_space=pltpu.HBM)] * 3,
        out_specs=(VMEM,) * 4,
        scratch_shapes=[
            pltpu.VMEM(metric_factor.shape, F32),
            pltpu.SemaphoreType.DMA((steps, machines // FETCH)),
            pltpu.SemaphoreType.DMA,
            pltpu.SemaphoreType.DMA,
        ],
        compiler_params=params(12),
    )(
        pltpu.with_memory_space_constraint(metric_factor, pltpu.HBM),
        pltpu.with_memory_space_constraint(tensor, pltpu.HBM),
        pltpu.with_memory_space_constraint(time_factor, pltpu.HBM),
    )
    gathered = lax.all_to_all(copies, "mach", 0, 0, axis_index_groups=plane_order).reshape(
        metrics // 2, 2 * RANK
    )
    half = own // 2
    partial, metric_block = pl.pallas_call(
        sums_kernel,
        out_shape=(
            jax.ShapeDtypeStruct((parts, half + GRAM, 2 * RANK), F32),
            jax.ShapeDtypeStruct((metrics, RANK), F32),
        ),
        in_specs=[VMEM] * 3,
        out_specs=(VMEM, VMEM),
        compiler_params=params(12),
    )(held, gathered, times)
    received = lax.all_to_all(partial, "met", 0, 0, axis_index_groups=[SUMS_ORDER])
    own_sums, gram = pl.pallas_call(
        reduce_kernel,
        out_shape=(
            jax.ShapeDtypeStruct((parts, half, 2 * RANK), F32),
            jax.ShapeDtypeStruct((GRAM, 2 * RANK), F32),
        ),
        in_specs=[VMEM],
        out_specs=(VMEM, VMEM),
        compiler_params=params(4),
    )(received)
    sums = lax.all_to_all(own_sums, "met", 0, 0, axis_index_groups=[ROWS_ORDER])
    weights, own_rows = pl.pallas_call(
        solve_kernel,
        out_shape=(
            jax.ShapeDtypeStruct((steps, 4 * RANK, metrics), BF16),
            jax.ShapeDtypeStruct((own, RANK), F32),
        ),
        in_specs=[VMEM] * 5,
        out_specs=(VMEM, VMEM),
        compiler_params=params(8),
        cost_estimate=work(10**9),
    )(gram, own_sums, metric_block, times, time_gram)
    residual = pl.pallas_call(
        residual_kernel,
        out_shape=jax.ShapeDtypeStruct(tensor.shape, F32),
        in_specs=[VMEM] * 3,
        out_specs=pl.BlockSpec(memory_space=pl.ANY),
        scratch_shapes=[
            pltpu.VMEM(tensor.shape, F32),
            pltpu.SemaphoreType.DMA((machines // PIECE, steps)),
        ],
        compiler_params=params(12),
    )(held, sums, weights)
    return own_rows, residual


def solution(mesh):
    def run(tensor, metric_factor, time_factor):
        return local(mesh.shape["met"], mesh.shape["mach"], tensor, metric_factor, time_factor)

    return jax.shard_map(
        run,
        mesh=mesh,
        in_specs=(P(None, "mach", "met"), P(("met", "mach"), None), P()),
        out_specs=(P(("mach", "met"), None), P(None, "mach", "met")),
        check_vma=False,
    )
```

```python
import jax
import jax.numpy as jnp
from jax import lax
from jax.experimental import pallas as pl
from jax.experimental.pallas import tpu as pltpu
from jax.sharding import PartitionSpec as P

RANK = 64
F32 = jnp.float32
BF16 = jnp.bfloat16
HIGHEST = lax.Precision.HIGHEST
VMEM = pl.BlockSpec(memory_space=pltpu.VMEM)
PIECE = 128
FETCH = 256
GRAM = 3 * RANK // 8
PLANE_FIRST = 37
SUMS_ORDER = (6, 7, 2, 3, 5, 0, 1, 4)
ROWS_ORDER = (6, 7, 3, 1, 0, 2, 5, 4)


def params(mebibytes):
    return pltpu.CompilerParams(vmem_limit_bytes=mebibytes * 1024 * 1024)


def work(flops):
    return pl.CostEstimate(flops=flops, bytes_accessed=10**7, transcendentals=0)


def split(x):
    high = x.astype(BF16)
    return high, (x - high.astype(F32)).astype(BF16)


def dot(a, b, contract, precision=None):
    return lax.dot_general(
        a, b, (contract, ((), ())), precision=precision, preferred_element_type=F32
    )


def begin_kernel(m_hbm, t_hbm, tf_hbm, out_ref, t_ref, tf_ref, gram_ref, m_ref, sems, m_sem, tf_sem):
    first = pltpu.make_async_copy(m_hbm, m_ref, m_sem)
    first.start()
    small = pltpu.make_async_copy(tf_hbm, tf_ref, tf_sem)
    small.start()
    copies = []
    steps, machines, _ = t_ref.shape
    for k in range(steps):
        for p in range(machines // FETCH):
            rows = pl.ds(p * FETCH, FETCH)
            copies.append(
                pltpu.make_async_copy(t_hbm.at[k, rows, :], t_ref.at[k, rows, :], sems.at[k, p])
            )
            copies[-1].start()
    first.wait()
    packed = jnp.concatenate(
        [
            jnp.concatenate([m_ref[i : i + 1, :], m_ref[i + 1 : i + 2, :]], axis=1)
            for i in range(0, m_ref.shape[0], 2)
        ],
        axis=0,
    )
    out_ref[...] = jnp.broadcast_to(packed[None], out_ref.shape)
    small.wait()
    tf = tf_ref[...]
    gram_ref[...] = dot(tf, tf, ((0,), (0,)), HIGHEST)
    for copy in copies:
        copy.wait()


def pack_gram(gram):
    half = RANK // 2
    rows = [gram[8 * i : 8 * i + 8] for i in range(RANK // 8)]
    return jnp.concatenate(
        [
            jnp.concatenate(rows[0:2], axis=1),
            jnp.concatenate(rows[2:4], axis=1),
            jnp.concatenate([row[:, half:] for row in rows[4:]], axis=1),
        ],
        axis=0,
    )


def unpack_gram(packed):
    half = RANK // 2
    top = jnp.concatenate(
        [packed[i : i + 8, h : h + RANK] for i in (0, 8) for h in (0, RANK)], axis=0
    )
    corner = jnp.concatenate(
        [packed[16:24, half * i : half * (i + 1)] for i in range(4)], axis=0
    )
    bottom = jnp.concatenate([top[:, half:].T, corner], axis=1)
    return jnp.concatenate([top, bottom], axis=0)


def sums_kernel(t_ref, g_ref, tf_ref, out_ref, m_ref):
    steps, machines, metrics = t_ref.shape
    parts = out_ref.shape[0]
    own = machines // parts
    half = own // 2
    cut = 2 * PLANE_FIRST
    top = metrics // 2 - cut
    pairs = g_ref[...]
    swapped = pltpu.roll(pairs, RANK, 1)
    left = lax.broadcasted_iota(jnp.int32, pairs.shape, 1) < RANK
    for h, rows in enumerate((jnp.where(left, pairs, swapped), jnp.where(left, swapped, pairs))):
        m_ref[pl.ds(2 * cut + h, top, stride=2), :] = rows[:top]
        m_ref[pl.ds(h, cut, stride=2), :] = rows[top:]
    m = m_ref[...]
    left = lax.broadcasted_iota(jnp.int32, m.shape, 1) < RANK
    factors = jnp.concatenate([tf_ref[...], tf_ref[...]], axis=1)
    acc = None
    for k in range(steps):
        high, low = split(m * factors[k : k + 1, :])
        right = jnp.where(left, high.astype(F32), low.astype(F32)).astype(BF16)
        high, low = split(t_ref[k])
        term = dot(high, right, ((1,), (0,))) + dot(low, right, ((1,), (0,)))
        acc = term if acc is None else acc + term
    once = m[:, :RANK]
    gram = pack_gram(dot(once, once, ((0,), (0,)), HIGHEST))
    left = lax.broadcasted_iota(jnp.int32, (half, 2 * RANK), 1) < RANK
    for i in range(parts):
        c = SUMS_ORDER[i]
        block = acc[c * own : (c + 1) * own]
        sums = block + pltpu.roll(block, RANK, 1)
        out_ref[i, :half, :] = jnp.where(left, sums[:half], sums[half:])
        out_ref[i, half:, :] = gram


def reduce_kernel(r_ref, own_ref, gram_ref):
    parts, rows, _ = own_ref.shape
    total = r_ref[0]
    for c in range(1, parts):
        total = total + r_ref[c]
    own_ref[...] = jnp.broadcast_to(total[None, :rows], own_ref.shape)
    gram_ref[...] = total[rows:]


def inverse_factor(normal):
    wide = 2 * RANK
    count = RANK // 8
    row_id = lax.broadcasted_iota(jnp.int32, (RANK, RANK), 0)
    col_id = lax.broadcasted_iota(jnp.int32, (RANK, RANK), 1)
    both = jnp.concatenate([normal, (row_id == col_id).astype(F32)], axis=1)
    blocks = [both[8 * b : 8 * b + 8] for b in range(count)]
    sub = lax.broadcasted_iota(jnp.int32, (8, wide), 0)

    def column(x, j):
        return jnp.broadcast_to(x[:, j : j + 1], (8, wide))

    def row(x, i):
        return jnp.broadcast_to(x[i : i + 1, :], (8, wide))

    done = []
    for b in range(count):
        panel = blocks[b]
        columns = [column(panel, 8 * b + t) for t in range(8)]
        entry = {(s, t): row(columns[t], s) for s in range(8) for t in range(s, 8)}
        upper = [row(panel, t) for t in range(8)]
        below = {
            i: [column(blocks[i], 8 * b + t) for t in range(8)] for i in range(b + 1, count)
        }
        rows = panel
        for s in range(0, 8, 2):
            v = s + 1
            a, o, d = entry[s, s], entry[s, v], entry[v, v]
            inverse = 1.0 / (a * d - o * o)
            later = range(s + 2, 8)
            first = {t: (entry[s, t] * d - entry[v, t] * o) * inverse for t in later}
            second = {t: (entry[v, t] * a - entry[s, t] * o) * inverse for t in later}
            upper_first = (upper[s] * d - upper[v] * o) * inverse
            upper_second = (upper[v] * a - upper[s] * o) * inverse
            for t in later:
                for q in range(t, 8):
                    entry[t, q] -= first[t] * entry[s, q] + second[t] * entry[v, q]
                upper[t] = upper[t] - (first[t] * upper[s] + second[t] * upper[v])
            for i, side in below.items():
                blocks[i] = blocks[i] - (side[s] * upper_first + side[v] * upper_second)
                for t in later:
                    side[t] = side[t] - (first[t] * side[s] + second[t] * side[v])
            ratio = o / a
            rows = jnp.where(sub == s, upper[s] * lax.rsqrt(a), rows)
            last = (upper[v] - ratio * upper[s]) * lax.rsqrt(d - o * ratio)
            rows = jnp.where(sub == v, last, rows)
        done.append(rows)
    return jnp.concatenate(done, axis=0)[:, RANK:]


def solve_kernel(gram_ref, own_ref, m_ref, tf_ref, times_ref, w_ref, rows_ref):
    inverse = inverse_factor(unpack_gram(gram_ref[...]) * times_ref[...])
    whole = dot(inverse, inverse, ((0,), (0,)), HIGHEST)
    sums = jnp.concatenate([own_ref[0, :, :RANK], own_ref[0, :, RANK:]], axis=0)
    rows_ref[...] = dot(sums, whole, ((1,), (0,)), HIGHEST)
    high, low = split(whole)
    left = jnp.concatenate([high, low, high, low], axis=1)
    m = m_ref[...]
    factors = jnp.concatenate([tf_ref[...], tf_ref[...]], axis=1)
    for k in range(tf_ref.shape[0]):
        right = jnp.concatenate(split(m * factors[k : k + 1, :]), axis=1)
        high, low = split(dot(left, right, ((1,), (1,))))
        w_ref[k] = jnp.concatenate([high, high, low, low], axis=0)


def residual_kernel(t_ref, s_ref, w_ref, out_ref, held, sems):
    parts, half, _ = s_ref.shape
    steps, machines, _ = t_ref.shape
    copies = []
    per = PIECE // (2 * half)
    for p in range(machines // PIECE):
        pieces = []
        for c in range(p * per, (p + 1) * per):
            block = s_ref[ROWS_ORDER.index(c)]
            pieces += [block[:, :RANK], block[:, RANK:]]
        high, low = split(jnp.concatenate(pieces, axis=0))
        left = jnp.concatenate([high, low, high, low], axis=1)
        rows = pl.ds(p * PIECE, PIECE)
        for k in range(steps):
            held[k, rows, :] = t_ref[k, rows, :] - dot(left, w_ref[k], ((1,), (0,)))
            copy = pltpu.make_async_copy(
                held.at[k, rows, :], out_ref.at[k, rows, :], sems.at[p, k]
            )
            copy.start()
            copies.append(copy)
    for copy in copies:
        copy.wait()


def local(parts, plane, tensor, metric_factor, time_factor):
    steps, machines, metrics = tensor.shape
    own = machines // parts
    rows = metric_factor.shape[0]
    plane_order = [[(i + PLANE_FIRST) % plane for i in range(plane)]]
    copies, held, times, time_gram = pl.pallas_call(
        begin_kernel,
        out_shape=(
            jax.ShapeDtypeStruct((plane, rows // 2, 2 * RANK), F32),
            jax.ShapeDtypeStruct(tensor.shape, F32),
            jax.ShapeDtypeStruct(time_factor.shape, F32),
            jax.ShapeDtypeStruct((RANK, RANK), F32),
        ),
        in_specs=[pl.BlockSpec(memory_space=pltpu.HBM)] * 3,
        out_specs=(VMEM,) * 4,
        scratch_shapes=[
            pltpu.VMEM(metric_factor.shape, F32),
            pltpu.SemaphoreType.DMA((steps, machines // FETCH)),
            pltpu.SemaphoreType.DMA,
            pltpu.SemaphoreType.DMA,
        ],
        compiler_params=params(12),
    )(
        pltpu.with_memory_space_constraint(metric_factor, pltpu.HBM),
        pltpu.with_memory_space_constraint(tensor, pltpu.HBM),
        pltpu.with_memory_space_constraint(time_factor, pltpu.HBM),
    )
    gathered = lax.all_to_all(copies, "mach", 0, 0, axis_index_groups=plane_order).reshape(
        metrics // 2, 2 * RANK
    )
    half = own // 2
    partial, metric_block = pl.pallas_call(
        sums_kernel,
        out_shape=(
            jax.ShapeDtypeStruct((parts, half + GRAM, 2 * RANK), F32),
            jax.ShapeDtypeStruct((metrics, 2 * RANK), F32),
        ),
        in_specs=[VMEM] * 3,
        out_specs=(VMEM, VMEM),
        compiler_params=params(12),
    )(held, gathered, times)
    received = lax.all_to_all(partial, "met", 0, 0, axis_index_groups=[SUMS_ORDER])
    own_sums, gram = pl.pallas_call(
        reduce_kernel,
        out_shape=(
            jax.ShapeDtypeStruct((parts, half, 2 * RANK), F32),
            jax.ShapeDtypeStruct((GRAM, 2 * RANK), F32),
        ),
        in_specs=[VMEM],
        out_specs=(VMEM, VMEM),
        compiler_params=params(4),
    )(received)
    sums = lax.all_to_all(own_sums, "met", 0, 0, axis_index_groups=[ROWS_ORDER])
    weights, own_rows = pl.pallas_call(
        solve_kernel,
        out_shape=(
            jax.ShapeDtypeStruct((steps, 4 * RANK, metrics), BF16),
            jax.ShapeDtypeStruct((own, RANK), F32),
        ),
        in_specs=[VMEM] * 5,
        out_specs=(VMEM, VMEM),
        compiler_params=params(8),
        cost_estimate=work(10**9),
    )(gram, own_sums, metric_block, times, time_gram)
    residual = pl.pallas_call(
        residual_kernel,
        out_shape=jax.ShapeDtypeStruct(tensor.shape, F32),
        in_specs=[VMEM] * 3,
        out_specs=pl.BlockSpec(memory_space=pl.ANY),
        scratch_shapes=[
            pltpu.VMEM(tensor.shape, F32),
            pltpu.SemaphoreType.DMA((machines // PIECE, steps)),
        ],
        compiler_params=params(12),
    )(held, sums, weights)
    return own_rows, residual


def solution(mesh):
    def run(tensor, metric_factor, time_factor):
        return local(mesh.shape["met"], mesh.shape["mach"], tensor, metric_factor, time_factor)

    return jax.shard_map(
        run,
        mesh=mesh,
        in_specs=(P(None, "mach", "met"), P(("met", "mach"), None), P()),
        out_specs=(P(("mach", "met"), None), P(None, "mach", "met")),
        check_vma=False,
    )
```

```python
import jax
import jax.numpy as jnp
from jax import lax
from jax.experimental import pallas as pl
from jax.experimental.pallas import tpu as pltpu
from jax.sharding import PartitionSpec as P

RANK = 64
F32 = jnp.float32
BF16 = jnp.bfloat16
HIGHEST = lax.Precision.HIGHEST
VMEM = pl.BlockSpec(memory_space=pltpu.VMEM)
PIECE = 128
FETCH = 256
GRAM = 3 * RANK // 8
PLANE_FIRST = 37
SUMS_ORDER = (6, 2, 7, 3, 5, 0, 1, 4)
ROWS_ORDER = (6, 7, 3, 5, 0, 2, 1, 4)


def params(mebibytes):
    return pltpu.CompilerParams(vmem_limit_bytes=mebibytes * 1024 * 1024)


def work(flops):
    return pl.CostEstimate(flops=flops, bytes_accessed=10**7, transcendentals=0)


def split(x):
    high = x.astype(BF16)
    return high, (x - high.astype(F32)).astype(BF16)


def dot(a, b, contract, precision=None):
    return lax.dot_general(
        a, b, (contract, ((), ())), precision=precision, preferred_element_type=F32
    )


def begin_kernel(m_hbm, t_hbm, tf_hbm, out_ref, t_ref, tf_ref, gram_ref, m_ref, sems, m_sem, tf_sem):
    first = pltpu.make_async_copy(m_hbm, m_ref, m_sem)
    first.start()
    small = pltpu.make_async_copy(tf_hbm, tf_ref, tf_sem)
    small.start()
    copies = []
    steps, machines, _ = t_ref.shape
    for k in range(steps):
        for p in range(machines // FETCH):
            rows = pl.ds(p * FETCH, FETCH)
            copies.append(
                pltpu.make_async_copy(t_hbm.at[k, rows, :], t_ref.at[k, rows, :], sems.at[k, p])
            )
            copies[-1].start()
    first.wait()
    packed = jnp.concatenate(
        [
            jnp.concatenate([m_ref[i : i + 1, :], m_ref[i + 1 : i + 2, :]], axis=1)
            for i in range(0, m_ref.shape[0], 2)
        ],
        axis=0,
    )
    out_ref[...] = jnp.broadcast_to(packed[None], out_ref.shape)
    small.wait()
    tf = tf_ref[...]
    gram_ref[...] = dot(tf, tf, ((0,), (0,)), HIGHEST)
    for copy in copies:
        copy.wait()


def pack_gram(gram):
    half = RANK // 2
    rows = [gram[8 * i : 8 * i + 8] for i in range(RANK // 8)]
    return jnp.concatenate(
        [
            jnp.concatenate(rows[0:2], axis=1),
            jnp.concatenate(rows[2:4], axis=1),
            jnp.concatenate([row[:, half:] for row in rows[4:]], axis=1),
        ],
        axis=0,
    )


def unpack_gram(packed):
    half = RANK // 2
    top = jnp.concatenate(
        [packed[i : i + 8, h : h + RANK] for i in (0, 8) for h in (0, RANK)], axis=0
    )
    corner = jnp.concatenate(
        [packed[16:24, half * i : half * (i + 1)] for i in range(4)], axis=0
    )
    bottom = jnp.concatenate([top[:, half:].T, corner], axis=1)
    return jnp.concatenate([top, bottom], axis=0)


def sums_kernel(t_ref, g_ref, tf_ref, out_ref, m_ref):
    steps, machines, metrics = t_ref.shape
    parts = out_ref.shape[0]
    own = machines // parts
    half = own // 2
    cut = 2 * PLANE_FIRST
    top = metrics // 2 - cut
    pairs = g_ref[...]
    swapped = pltpu.roll(pairs, RANK, 1)
    left = lax.broadcasted_iota(jnp.int32, pairs.shape, 1) < RANK
    for h, rows in enumerate((jnp.where(left, pairs, swapped), jnp.where(left, swapped, pairs))):
        m_ref[pl.ds(2 * cut + h, top, stride=2), :] = rows[:top]
        m_ref[pl.ds(h, cut, stride=2), :] = rows[top:]
    m = m_ref[...]
    left = lax.broadcasted_iota(jnp.int32, m.shape, 1) < RANK
    factors = jnp.concatenate([tf_ref[...], tf_ref[...]], axis=1)
    acc = None
    for k in range(steps):
        high, low = split(m * factors[k : k + 1, :])
        right = jnp.where(left, high.astype(F32), low.astype(F32)).astype(BF16)
        high, low = split(t_ref[k])
        term = dot(high, right, ((1,), (0,))) + dot(low, right, ((1,), (0,)))
        acc = term if acc is None else acc + term
    once = m[:, :RANK]
    gram = pack_gram(dot(once, once, ((0,), (0,)), HIGHEST))
    left = lax.broadcasted_iota(jnp.int32, (half, 2 * RANK), 1) < RANK
    for i in range(parts):
        c = SUMS_ORDER[i]
        block = acc[c * own : (c + 1) * own]
        sums = block + pltpu.roll(block, RANK, 1)
        out_ref[i, :half, :] = jnp.where(left, sums[:half], sums[half:])
        out_ref[i, half:, :] = gram


def reduce_kernel(r_ref, own_ref, gram_ref):
    parts, rows, _ = own_ref.shape
    total = r_ref[0]
    for c in range(1, parts):
        total = total + r_ref[c]
    own_ref[...] = jnp.broadcast_to(total[None, :rows], own_ref.shape)
    gram_ref[...] = total[rows:]


def inverse_factor(normal):
    wide = 2 * RANK
    count = RANK // 8
    row_id = lax.broadcasted_iota(jnp.int32, (RANK, RANK), 0)
    col_id = lax.broadcasted_iota(jnp.int32, (RANK, RANK), 1)
    both = jnp.concatenate([normal, (row_id == col_id).astype(F32)], axis=1)
    blocks = [both[8 * b : 8 * b + 8] for b in range(count)]
    sub = lax.broadcasted_iota(jnp.int32, (8, wide), 0)

    def column(x, j):
        return jnp.broadcast_to(x[:, j : j + 1], (8, wide))

    def row(x, i):
        return jnp.broadcast_to(x[i : i + 1, :], (8, wide))

    done = []
    for b in range(count):
        panel = blocks[b]
        columns = [column(panel, 8 * b + t) for t in range(8)]
        entry = {(s, t): row(columns[t], s) for s in range(8) for t in range(s, 8)}
        upper = [row(panel, t) for t in range(8)]
        below = {
            i: [column(blocks[i], 8 * b + t) for t in range(8)] for i in range(b + 1, count)
        }
        rows = panel
        for s in range(0, 8, 2):
            v = s + 1
            a, o, d = entry[s, s], entry[s, v], entry[v, v]
            inverse = 1.0 / (a * d - o * o)
            later = range(s + 2, 8)
            first = {t: (entry[s, t] * d - entry[v, t] * o) * inverse for t in later}
            second = {t: (entry[v, t] * a - entry[s, t] * o) * inverse for t in later}
            upper_first = (upper[s] * d - upper[v] * o) * inverse
            upper_second = (upper[v] * a - upper[s] * o) * inverse
            for t in later:
                for q in range(t, 8):
                    entry[t, q] -= first[t] * entry[s, q] + second[t] * entry[v, q]
                upper[t] = upper[t] - (first[t] * upper[s] + second[t] * upper[v])
            for i, side in below.items():
                blocks[i] = blocks[i] - (side[s] * upper_first + side[v] * upper_second)
                for t in later:
                    side[t] = side[t] - (first[t] * side[s] + second[t] * side[v])
            ratio = o / a
            rows = jnp.where(sub == s, upper[s] * lax.rsqrt(a), rows)
            last = (upper[v] - ratio * upper[s]) * lax.rsqrt(d - o * ratio)
            rows = jnp.where(sub == v, last, rows)
        done.append(rows)
    return jnp.concatenate(done, axis=0)[:, RANK:]


def solve_kernel(gram_ref, own_ref, m_ref, tf_ref, times_ref, w_ref, rows_ref):
    inverse = inverse_factor(unpack_gram(gram_ref[...]) * times_ref[...])
    whole = dot(inverse, inverse, ((0,), (0,)), HIGHEST)
    sums = jnp.concatenate([own_ref[0, :, :RANK], own_ref[0, :, RANK:]], axis=0)
    rows_ref[...] = dot(sums, whole, ((1,), (0,)), HIGHEST)
    high, low = split(whole)
    left = jnp.concatenate([high, low, high, low], axis=1)
    m = m_ref[...]
    factors = jnp.concatenate([tf_ref[...], tf_ref[...]], axis=1)
    for k in range(tf_ref.shape[0]):
        right = jnp.concatenate(split(m * factors[k : k + 1, :]), axis=1)
        high, low = split(dot(left, right, ((1,), (1,))))
        w_ref[k] = jnp.concatenate([high, high, low, low], axis=0)


def residual_kernel(t_ref, s_ref, w_ref, out_ref, held, sems):
    parts, half, _ = s_ref.shape
    steps, machines, _ = t_ref.shape
    copies = []
    per = PIECE // (2 * half)
    for p in range(machines // PIECE):
        pieces = []
        for c in range(p * per, (p + 1) * per):
            block = s_ref[ROWS_ORDER.index(c)]
            pieces += [block[:, :RANK], block[:, RANK:]]
        high, low = split(jnp.concatenate(pieces, axis=0))
        left = jnp.concatenate([high, low, high, low], axis=1)
        rows = pl.ds(p * PIECE, PIECE)
        for k in range(steps):
            held[k, rows, :] = t_ref[k, rows, :] - dot(left, w_ref[k], ((1,), (0,)))
            copy = pltpu.make_async_copy(
                held.at[k, rows, :], out_ref.at[k, rows, :], sems.at[p, k]
            )
            copy.start()
            copies.append(copy)
    for copy in copies:
        copy.wait()


def local(parts, plane, tensor, metric_factor, time_factor):
    steps, machines, metrics = tensor.shape
    own = machines // parts
    rows = metric_factor.shape[0]
    plane_order = [[(i + PLANE_FIRST) % plane for i in range(plane)]]
    copies, held, times, time_gram = pl.pallas_call(
        begin_kernel,
        out_shape=(
            jax.ShapeDtypeStruct((plane, rows // 2, 2 * RANK), F32),
            jax.ShapeDtypeStruct(tensor.shape, F32),
            jax.ShapeDtypeStruct(time_factor.shape, F32),
            jax.ShapeDtypeStruct((RANK, RANK), F32),
        ),
        in_specs=[pl.BlockSpec(memory_space=pltpu.HBM)] * 3,
        out_specs=(VMEM,) * 4,
        scratch_shapes=[
            pltpu.VMEM(metric_factor.shape, F32),
            pltpu.SemaphoreType.DMA((steps, machines // FETCH)),
            pltpu.SemaphoreType.DMA,
            pltpu.SemaphoreType.DMA,
        ],
        compiler_params=params(12),
    )(
        pltpu.with_memory_space_constraint(metric_factor, pltpu.HBM),
        pltpu.with_memory_space_constraint(tensor, pltpu.HBM),
        pltpu.with_memory_space_constraint(time_factor, pltpu.HBM),
    )
    gathered = lax.all_to_all(copies, "mach", 0, 0, axis_index_groups=plane_order).reshape(
        metrics // 2, 2 * RANK
    )
    half = own // 2
    partial, metric_block = pl.pallas_call(
        sums_kernel,
        out_shape=(
            jax.ShapeDtypeStruct((parts, half + GRAM, 2 * RANK), F32),
            jax.ShapeDtypeStruct((metrics, 2 * RANK), F32),
        ),
        in_specs=[VMEM] * 3,
        out_specs=(VMEM, VMEM),
        compiler_params=params(12),
    )(held, gathered, times)
    received = lax.all_to_all(partial, "met", 0, 0, axis_index_groups=[SUMS_ORDER])
    own_sums, gram = pl.pallas_call(
        reduce_kernel,
        out_shape=(
            jax.ShapeDtypeStruct((parts, half, 2 * RANK), F32),
            jax.ShapeDtypeStruct((GRAM, 2 * RANK), F32),
        ),
        in_specs=[VMEM],
        out_specs=(VMEM, VMEM),
        compiler_params=params(4),
    )(received)
    sums = lax.all_to_all(own_sums, "met", 0, 0, axis_index_groups=[ROWS_ORDER])
    weights, own_rows = pl.pallas_call(
        solve_kernel,
        out_shape=(
            jax.ShapeDtypeStruct((steps, 4 * RANK, metrics), BF16),
            jax.ShapeDtypeStruct((own, RANK), F32),
        ),
        in_specs=[VMEM] * 5,
        out_specs=(VMEM, VMEM),
        compiler_params=params(8),
        cost_estimate=work(10**9),
    )(gram, own_sums, metric_block, times, time_gram)
    residual = pl.pallas_call(
        residual_kernel,
        out_shape=jax.ShapeDtypeStruct(tensor.shape, F32),
        in_specs=[VMEM] * 3,
        out_specs=pl.BlockSpec(memory_space=pl.ANY),
        scratch_shapes=[
            pltpu.VMEM(tensor.shape, F32),
            pltpu.SemaphoreType.DMA((machines // PIECE, steps)),
        ],
        compiler_params=params(12),
    )(held, sums, weights)
    return own_rows, residual


def solution(mesh):
    def run(tensor, metric_factor, time_factor):
        return local(mesh.shape["met"], mesh.shape["mach"], tensor, metric_factor, time_factor)

    return jax.shard_map(
        run,
        mesh=mesh,
        in_specs=(P(None, "mach", "met"), P(("met", "mach"), None), P()),
        out_specs=(P(("mach", "met"), None), P(None, "mach", "met")),
        check_vma=False,
    )
```
